32 devices in a mesh: dp: 4 (over x, core), expert: 8 (over z, y).
Axes of the slice: x: 2, y: 2, z: 4, core: 2. Of those that a mesh axis runs over, the one named last changes fastest.
Arguments:
- tokens_in: bfloat16 [4096, 2048], P(('dp', 'expert')), may hold values from -6 to 6
- out_grad: bfloat16 [4096, 2048], P(('dp', 'expert')), may hold values from -6 to 6
- gate_logits: float32 [4096, 8], P(('dp', 'expert')), may hold values from -6 to 6
- route_ids: int32 [4096, 8], P(('dp', 'expert')), may hold values from 0 to 15, all different within a row; in each aligned block of 128 rows (0 to 127, 128 to 255, ...) at most 72 rows name the same one
- w_gate: bfloat16 [2048, 16, 768], P(None, 'expert'), may hold values from -0.125 to 0.125
- w_up: bfloat16 [2048, 16, 768], P(None, 'expert'), may hold values from -0.125 to 0.125
- w_down: bfloat16 [2048, 16, 768], P(None, 'expert'), may hold values from -0.21875 to 0.21875
Outputs:
- input_grad: bfloat16 [4096, 2048], P(('dp', 'expert'))
- router_grad: float32 [4096, 8], P(('dp', 'expert'))
- weight_grads: bfloat16 [2048, 3, 16, 768], P('dp', None, 'expert')
The draws below stay inside these ranges and needn't reach their ends.
Inputs may be any that keep to these rules, and one draw needn't show every extreme that they name: `route_ids`: the 8 experts of a token differ. In each aligned block of 128 rows (the rows of one device) no expert is named by more than 72 rows, a bound that some block reaches.
All inputs are finite; a program needn't handle non-finite values.
Results may differ from the reference program's by a relative error of at most 0.015.
Values may be sent and summed in bfloat16 or wider, within the bound.
A program may use at most 192 MiB of HBM per device.

```python
import math
import jax
import jax.numpy as jnp
import numpy as np
from jax import lax

D = 2048
H = 768
TOPK = 8
TOK_DEV = 128
EXPERTS = 16
MOST = 72
TOKENS = 4096
N_DP = 4


def steps_of(key, shape, split, low, high):
    level = 1.0
    for axis_at, shards_of in split:
        draws = jax.random.uniform(jax.random.fold_in(jax.random.fold_in(key, 6), axis_at), (shards_of,), jnp.float32, low / len(split), high / len(split))
        level = level * jnp.repeat(jnp.exp(draws), shape[axis_at] // shards_of).reshape((-1,) + (1,) * (len(shape) - 1 - axis_at))
    return level


def routed_block(key, own, number, rows, count, top, limit, skew):
    order = jax.random.permutation(key, count)
    heavy_load, ordinary = portions_of(count, rows * top, limit, skew, True), portions_of(count, rows * top, limit, skew, False)
    places = jnp.arange(count)

    def named(lengths, rotation):
        used = int((lengths > 0).sum())
        fixed = max(1, used // 4)
        moved = fixed + (places - fixed + rotation * (used - fixed)) % max(1, count - fixed)
        return jnp.zeros((count,), jnp.int32).at[order[jnp.where(places < fixed, places, moved)]].set(jnp.asarray(lengths, jnp.int32))

    lengths = jnp.where(number % 4 == 0, named(heavy_load, number // 4), named(ordinary, number - number // 4 - 1))
    mixed = jax.random.permutation(jax.random.fold_in(own, 3), count)
    source_of, receiver = mixed[0:count // 2 * 2:2], mixed[1:count // 2 * 2:2]
    margin = jnp.minimum(lengths[source_of] - 1, limit - lengths[receiver]) // 2
    margin = jnp.where((source_of == order[0]) | (receiver == order[0]) | (lengths[receiver] == 0), 0, jnp.maximum(margin, 0))
    moved = jax.random.randint(jax.random.fold_in(own, 4), (count // 2,), 0, 1 << 20) % (margin + 1)
    lengths = lengths.at[source_of].add(-moved).at[receiver].add(moved)
    items = jnp.searchsorted(jnp.cumsum(lengths), jnp.arange(rows * top), side="right").astype(jnp.int32)
    grid = items.reshape(top, rows).T
    grid = grid[jax.random.permutation(jax.random.fold_in(own, 1), rows)]
    rotation = jax.random.randint(jax.random.fold_in(own, 2), (rows, 1), 0, top)
    return jnp.take_along_axis(grid, (jnp.arange(top)[None, :] + rotation) % top, axis=1)


def portions_of(number_of, total, bound, slope, full):
    loads = [(1 << 20) // math.isqrt(standing ** slope) + 1 for standing in range(1, number_of + 1)]
    largest = bound if full else min(bound, max(-(-total // number_of), total * loads[0] // sum(loads)))
    least = 1 if total - largest >= number_of - 1 else 0
    holding, spare = [largest] + [least] * (number_of - 1), total - largest - least * (number_of - 1)
    while spare > 0:
        candidates = [i for i in range(1, number_of) if holding[i] < largest] or [i for i in range(1, number_of) if holding[i] < bound]
        pool, left = sum([loads[i] for i in candidates]), spare
        for i in candidates:
            more = min(bound - holding[i], max(1, left * loads[i] // pool), spare)
            holding[i] = holding[i] + more
            spare = spare - more
    return np.array(holding)


def noise(key, shape, width, reach, split=(), held_as=jnp.bfloat16):
    gain = steps_of(key, shape, split, -0.22, 0.18) if split else 1.0
    entries = jax.random.normal(key, shape, jnp.float32) * width * gain
    return jnp.minimum(jnp.maximum(entries, -reach), reach).astype(held_as)


def setup_inputs(seed: int = 0) -> dict:
    streams_of = jax.random.split(jax.random.key(seed), 8)
    tokens_in = noise(streams_of[0], (TOKENS, D), 1.0, 6.0, ((0, 32),))
    out_grad = noise(streams_of[1], (TOKENS, D), 1.0, 6.0, ((0, 32),))
    gate_logits = noise(streams_of[2], (TOKENS, TOPK), 1.5, 6.0, ((0, 32),), jnp.float32)
    route_ids_keys = jax.random.split(jax.random.fold_in(streams_of[3], 1), TOKENS // TOK_DEV)
    route_ids_turns = jax.random.permutation(jax.random.fold_in(streams_of[3], 3), TOKENS // TOK_DEV)
    route_ids = jax.vmap(lambda own, number: routed_block(jax.random.fold_in(streams_of[3], 2), own, number, TOK_DEV, EXPERTS, TOPK, MOST, 2))(route_ids_keys, route_ids_turns).reshape((TOKENS, TOPK))
    w_gate = noise(streams_of[4], (D, EXPERTS, H), D ** -0.5, 0.125, ((1, 8),))
    w_up = noise(streams_of[5], (D, EXPERTS, H), D ** -0.5, 0.125, ((1, 8),))
    w_down = noise(streams_of[6], (D, EXPERTS, H), H ** -0.5, 0.21875, ((1, 8),))
    return dict(tokens_in=tokens_in, out_grad=out_grad, gate_logits=gate_logits, route_ids=route_ids, w_gate=w_gate, w_up=w_up, w_down=w_down)


def combine_weights(gate_logits):
    raised = jnp.exp(gate_logits)
    return raised / lax.optimization_barrier(jnp.sum(raised, axis=1, keepdims=True))

def group_grad(left, right):
    parts = jnp.einsum('gmd,gmh->gdh', left.reshape(N_DP, -1, left.shape[1]).astype(jnp.float32), right.reshape(N_DP, -1, right.shape[1]).astype(jnp.float32), precision=lax.Precision.HIGHEST)
    return parts

def reference(tokens_in, out_grad, gate_logits, route_ids, w_gate, w_up, w_down):
    tok_total = tokens_in.shape[0]
    pair_count = tok_total * TOPK
    block_count = tok_total // TOK_DEV
    weights = combine_weights(gate_logits)
    scaled = (weights[:, :, None] * out_grad[:, None, :].astype(jnp.float32)).astype(jnp.bfloat16)
    scaled = scaled.reshape(pair_count, D)
    flat_ids = route_ids.reshape(-1).astype(jnp.int32)
    block_ids = flat_ids.reshape(block_count, TOK_DEV * TOPK)
    onehot = (block_ids[:, :, None] == jnp.arange(EXPERTS, dtype=jnp.int32)[None, None, :]).astype(jnp.int32)
    before = jnp.cumsum(onehot, axis=1) - onehot
    slot_rank = lax.optimization_barrier(jnp.sum(before * onehot, axis=2)).reshape(-1)
    block_of_pair = jnp.arange(pair_count, dtype=jnp.int32) // (TOK_DEV * TOPK)
    table_pos = flat_ids * (block_count * MOST) + block_of_pair * MOST + slot_rank
    slot_table = jnp.full((EXPERTS * block_count * MOST,), pair_count, jnp.int32)
    slot_table = slot_table.at[table_pos].set(jnp.arange(pair_count, dtype=jnp.int32))
    slot_table = slot_table.reshape(EXPERTS, block_count * MOST)
    zero_row = jnp.zeros((1, D), jnp.bfloat16)
    token_table = jnp.concatenate([tokens_in, zero_row], axis=0)
    scaled_table = jnp.concatenate([scaled, zero_row], axis=0)

    def per_expert(running, inputs):
        rows_grad, probs_all = running
        slot_index, gate_matrix, up_matrix, down_matrix = inputs
        token_index = (slot_index // TOPK).astype(jnp.int32)
        row_tokens = jnp.take(token_table, token_index, axis=0)
        row_scaled = jnp.take(scaled_table, slot_index, axis=0)
        gate_pre = jnp.dot(row_tokens, gate_matrix, preferred_element_type=jnp.float32)
        up_pre = jnp.dot(row_tokens, up_matrix, preferred_element_type=jnp.float32)
        sigmoid_gate = jax.nn.sigmoid(gate_pre)
        active = gate_pre * sigmoid_gate
        hidden = (active * up_pre).astype(jnp.bfloat16)
        hidden_grad = jnp.dot(row_scaled, down_matrix, preferred_element_type=jnp.float32)
        prob_part = lax.optimization_barrier(jnp.sum(hidden_grad * hidden.astype(jnp.float32), axis=1)).astype(jnp.bfloat16)
        gate_grad = (hidden_grad * up_pre * sigmoid_gate * (1.0 + gate_pre * (1.0 - sigmoid_gate))).astype(jnp.bfloat16)
        up_grad = (hidden_grad * active).astype(jnp.bfloat16)
        row_grad = (jnp.dot(gate_grad, gate_matrix.T, preferred_element_type=jnp.float32) + jnp.dot(up_grad, up_matrix.T, preferred_element_type=jnp.float32)).astype(jnp.bfloat16)
        group_parts = jnp.stack([group_grad(row_tokens, gate_grad), group_grad(row_tokens, up_grad), group_grad(row_scaled, hidden)], axis=2)
        rounded_parts = lax.optimization_barrier(group_parts.astype(jnp.bfloat16)).astype(jnp.float32)
        matrix_grads = lax.optimization_barrier(jnp.sum(rounded_parts, axis=0)).astype(jnp.bfloat16)
        rows_grad = rows_grad.at[slot_index].set(row_grad)
        probs_all = probs_all.at[slot_index].set(prob_part)
        return ((rows_grad, probs_all), matrix_grads)
    initial = (jnp.zeros((pair_count + 1, D), jnp.bfloat16), jnp.zeros((pair_count + 1,), jnp.bfloat16))
    matrices = (slot_table, jnp.moveaxis(w_gate, 1, 0), jnp.moveaxis(w_up, 1, 0), jnp.moveaxis(w_down, 1, 0))
    (rows_grad, probs_all), grads = lax.scan(per_expert, initial, matrices)
    input_grad = lax.optimization_barrier(jnp.sum(rows_grad[:pair_count].reshape(tok_total, TOPK, D).astype(jnp.float32), axis=1)).astype(jnp.bfloat16)
    prob_part = probs_all[:pair_count].reshape(tok_total, TOPK).astype(jnp.float32)
    router_grad = prob_part - weights * lax.optimization_barrier(jnp.sum(prob_part, axis=1, keepdims=True))
    weight_grads = jnp.transpose(grads, (1, 2, 0, 3))
    return (input_grad, router_grad, weight_grads)
```

```python
import jax
import jax.numpy as jnp
from jax import lax
from jax.sharding import PartitionSpec as P

BF16 = jnp.bfloat16
F32 = jnp.float32


def combine_weights(gate_logits):
    raised = jnp.exp(gate_logits)
    return raised / jnp.sum(raised, axis=1, keepdims=True)


def per_device(tokens_in, out_grad, gate_logits, route_ids, w_gate, w_up, w_down):
    tok_rows, model_width = tokens_in.shape
    topk_count = route_ids.shape[1]
    local_experts = w_gate.shape[1]
    hidden_width = w_gate.shape[2]
    owners = lax.axis_size("expert")
    expert_count = local_experts * owners
    capacity = 9 * tok_rows * topk_count // (8 * expert_count)
    row_count = owners * capacity
    weights = combine_weights(gate_logits)

    meta = jnp.concatenate([weights, route_ids.astype(F32)], axis=1)
    meta = lax.all_gather(meta, "expert", axis=0)
    all_tokens = lax.all_gather(tokens_in, "expert", axis=0)
    all_grads = lax.all_gather(out_grad, "expert", axis=0)

    w_gu = lax.optimization_barrier(
        jnp.concatenate([jnp.transpose(w_gate, (1, 0, 2)), jnp.transpose(w_up, (1, 0, 2))], axis=2)
    )
    w_dn = lax.optimization_barrier(jnp.transpose(w_down, (1, 0, 2)))

    all_weights = meta[:, :, :topk_count]
    all_ids = meta[:, :, topk_count:].astype(jnp.int32)
    mine = lax.axis_index("expert") * local_experts + jnp.arange(local_experts, dtype=jnp.int32)
    hit = all_ids[:, None, :, :] == mine[None, :, None, None]
    named = jnp.any(hit, axis=3)
    pair_weight = jnp.sum(jnp.where(hit, all_weights[:, None], 0.0), axis=3)
    earlier = (
        jnp.arange(tok_rows, dtype=jnp.int32)[:, None]
        < jnp.arange(tok_rows, dtype=jnp.int32)[None, :]
    ).astype(BF16)
    rank = jnp.einsum("nes,st->net", named.astype(BF16), earlier, preferred_element_type=F32)
    rank = jnp.where(named, rank.astype(jnp.int32), -1)
    chosen = rank[:, :, None, :] == jnp.arange(capacity, dtype=jnp.int32)[None, None, :, None]
    select = lax.optimization_barrier(chosen.astype(BF16))
    slot_weight = jnp.sum(jnp.where(chosen, pair_weight[:, :, None, :], 0.0), axis=3)

    def dispatch(blocks):
        return jnp.einsum("nect,ntd->necd", select, blocks, preferred_element_type=F32)

    def expert_major(rows):
        return jnp.transpose(rows, (1, 0, 2, 3)).reshape(local_experts, row_count, rows.shape[3])

    rows_in = expert_major(dispatch(all_tokens).astype(BF16))
    pre = jnp.einsum("emd,edh->emh", rows_in, w_gu, preferred_element_type=F32)
    gate_pre, up_pre = pre[:, :, :hidden_width], pre[:, :, hidden_width:]
    sigmoid_gate = jax.nn.sigmoid(gate_pre)
    active = gate_pre * sigmoid_gate
    hidden = (active * up_pre).astype(BF16)

    rows_scaled = expert_major(
        (slot_weight[:, :, :, None] * dispatch(all_grads)).astype(BF16)
    )
    hidden_grad = jnp.einsum("emd,edh->emh", rows_scaled, w_dn, preferred_element_type=F32)
    grad_down = jnp.einsum("emd,emh->edh", rows_scaled, hidden, preferred_element_type=F32)
    share_down = lax.psum_scatter(grad_down.astype(BF16), "dp", scatter_dimension=1, tiled=True)
    prob_part = jnp.sum(hidden_grad * hidden.astype(F32), axis=2).astype(BF16)
    gate_grad = (
        hidden_grad * up_pre * sigmoid_gate * (1.0 + gate_pre * (1.0 - sigmoid_gate))
    ).astype(BF16)
    up_grad = (hidden_grad * active).astype(BF16)
    both_grad = jnp.concatenate([gate_grad, up_grad], axis=2)
    grad_both = jnp.einsum("emd,emh->edh", rows_in, both_grad, preferred_element_type=F32)
    share_both = lax.psum_scatter(grad_both.astype(BF16), "dp", scatter_dimension=1, tiled=True)

    row_grad = jnp.einsum("emh,edh->emd", both_grad, w_gu, preferred_element_type=F32).astype(BF16)
    row_grad = row_grad.reshape(local_experts, owners, capacity, model_width)
    partial = jnp.einsum("nect,encd->ntd", select, row_grad, preferred_element_type=F32)
    input_grad = lax.psum_scatter(
        partial.astype(BF16).reshape(owners * tok_rows, model_width),
        "expert",
        scatter_dimension=0,
        tiled=True,
    )
    slot_prob = prob_part.astype(F32).reshape(local_experts, owners, capacity)
    slot_prob = jnp.transpose(slot_prob, (1, 0, 2))
    token_prob = jnp.sum(jnp.where(chosen, slot_prob[:, :, :, None], 0.0), axis=2)
    probs = jnp.sum(jnp.where(hit, token_prob[:, :, :, None], 0.0), axis=1)
    pair_probs = lax.psum_scatter(
        probs.reshape(owners * tok_rows, topk_count), "expert", scatter_dimension=0, tiled=True
    )
    router_grad = pair_probs - weights * jnp.sum(pair_probs, axis=1, keepdims=True)

    shares = jnp.stack(
        [share_both[:, :, :hidden_width], share_both[:, :, hidden_width:], share_down], axis=0
    )
    return (input_grad, router_grad, jnp.transpose(shares, (2, 0, 1, 3)))


def solution(mesh):
    rows = P(("dp", "expert"), None)
    experts = P(None, "expert", None)
    in_specs = (rows, rows, rows, rows, experts, experts, experts)
    out_specs = (rows, rows, P("dp", None, "expert", None))
    return jax.shard_map(
        per_device, mesh=mesh, in_specs=in_specs, out_specs=out_specs, check_vma=False
    )
```

```python
import jax
import jax.numpy as jnp
from jax import lax
from jax.sharding import PartitionSpec as P

BF16 = jnp.bfloat16
F32 = jnp.float32


def combine_weights(gate_logits):
    raised = jnp.exp(gate_logits)
    return raised / jnp.sum(raised, axis=1, keepdims=True)

LINE = 4


def add(*terms):
    total = terms[0].astype(F32)
    for term in terms[1:]:
        total = total + term.astype(F32)
    return total


def gather_blocks(block, owners):
    if owners != 2 * LINE:
        return lax.all_gather(block, "expert", axis=0)
    place = lax.axis_index("expert") // 2
    ups, downs = [block], [block]
    for step in range(1, LINE):
        up = [(i, i + 2) for i in range(owners - 2) if i // 2 >= step - 1]
        down = [(i, i - 2) for i in range(2, owners) if LINE - 1 - i // 2 >= step - 1]
        ups.append(lax.ppermute(ups[-1], "expert", up))
        downs.append(lax.ppermute(downs[-1], "expert", down))
    column = [block]
    for step in range(1, LINE):
        column.append(jnp.where(place >= step, ups[step], downs[LINE - step]))
    swap = [(i, i ^ 1) for i in range(owners)]
    return jnp.stack(column + [lax.ppermute(one, "expert", swap) for one in column])


def scatter_blocks(part_of, owners, dtype):
    if owners != 2 * LINE:
        parts = part_of(list(range(owners))).astype(dtype)
        return lax.psum_scatter(parts, "expert", scatter_dimension=0, tiled=False)
    swap = [(i, i ^ 1) for i in range(owners)]
    column = {}
    for pair in ((1, 3), (2, 0)):
        there = part_of([LINE + one for one in pair]).astype(dtype)
        back = lax.ppermute(there, "expert", swap)
        both = add(part_of(list(pair)), back)
        column[pair[0]], column[pair[1]] = both[0], both[1]
    ups, downs = None, None
    for step in range(1, LINE):
        up = [(i, i + 2) for i in range(owners - 2) if i // 2 + LINE - step <= LINE - 1]
        down = [(i, i - 2) for i in range(2, owners) if i // 2 >= LINE - step]
        send_up = column[step] if ups is None else add(column[step], ups)
        send_down = column[LINE - step] if downs is None else add(column[LINE - step], downs)
        ups = lax.ppermute(send_up.astype(dtype), "expert", up)
        downs = lax.ppermute(send_down.astype(dtype), "expert", down)
    return add(column[0], ups, downs).astype(dtype)


def reduced_product(rows, grads):
    group = lax.axis_index("dp")
    chip, core = group // 2, group % 2
    width = rows.shape[2] // 4

    def product(to_chip, to_core):
        start = (to_chip * 2 + to_core) * width
        part = lax.dynamic_slice_in_dim(rows, start, width, axis=2)
        return jnp.einsum("emd,emh->edh", part, grads, preferred_element_type=F32)

    def over_core(part):
        return lax.ppermute(part.astype(BF16), "dp", [(0, 1), (1, 0), (2, 3), (3, 2)])

    def over_chip(part):
        return lax.ppermute(part.astype(BF16), "dp", [(0, 2), (2, 0), (1, 3), (3, 1)])

    far = over_core(product(1 - chip, 1 - core))
    near = over_core(product(chip, 1 - core))
    far = over_chip(add(product(1 - chip, core), far))
    return add(product(chip, core), near, far).astype(BF16)


def per_device(tokens_in, out_grad, gate_logits, route_ids, w_gate, w_up, w_down):
    tok_rows, model_width = tokens_in.shape
    topk_count = route_ids.shape[1]
    local_experts = w_gate.shape[1]
    hidden_width = w_gate.shape[2]
    owners = lax.axis_size("expert")
    expert_count = local_experts * owners
    capacity = 9 * tok_rows * topk_count // (8 * expert_count)
    row_count = owners * capacity
    weights = combine_weights(gate_logits)

    meta = jnp.concatenate([weights.T, route_ids.T.astype(F32)], axis=0)
    meta = jnp.transpose(gather_blocks(meta, owners), (0, 2, 1))
    all_tokens = gather_blocks(tokens_in, owners)
    all_grads = gather_blocks(out_grad, owners)

    w_gu = lax.optimization_barrier(
        jnp.concatenate([jnp.transpose(w_gate, (1, 0, 2)), jnp.transpose(w_up, (1, 0, 2))], axis=2)
    )
    w_dn = lax.optimization_barrier(jnp.transpose(w_down, (1, 0, 2)))

    all_weights = meta[:, :, :topk_count]
    all_ids = meta[:, :, topk_count:].astype(jnp.int32)
    mine = lax.axis_index("expert") * local_experts + jnp.arange(local_experts, dtype=jnp.int32)
    hit = all_ids[:, None, :, :] == mine[None, :, None, None]
    named = jnp.any(hit, axis=3)
    pair_weight = jnp.sum(jnp.where(hit, all_weights[:, None], 0.0), axis=3)
    earlier = (
        jnp.arange(tok_rows, dtype=jnp.int32)[:, None]
        < jnp.arange(tok_rows, dtype=jnp.int32)[None, :]
    ).astype(BF16)
    rank = jnp.einsum("nes,st->net", named.astype(BF16), earlier, preferred_element_type=F32)
    rank = jnp.where(named, rank.astype(jnp.int32), -1)
    chosen = rank[:, :, None, :] == jnp.arange(capacity, dtype=jnp.int32)[None, None, :, None]
    select = lax.optimization_barrier(chosen.astype(BF16))
    slot_weight = jnp.sum(jnp.where(chosen, pair_weight[:, :, None, :], 0.0), axis=3)

    def dispatch(blocks):
        return jnp.einsum("nect,ntd->necd", select, blocks, preferred_element_type=F32)

    def expert_major(rows):
        return jnp.transpose(rows, (1, 0, 2, 3)).reshape(local_experts, row_count, rows.shape[3])

    rows_in = expert_major(dispatch(all_tokens).astype(BF16))
    pre = jnp.einsum("emd,edh->emh", rows_in, w_gu, preferred_element_type=F32)
    gate_pre, up_pre = pre[:, :, :hidden_width], pre[:, :, hidden_width:]
    sigmoid_gate = jax.nn.sigmoid(gate_pre)
    active = gate_pre * sigmoid_gate
    hidden = (active * up_pre).astype(BF16)

    rows_scaled = expert_major(
        (slot_weight[:, :, :, None] * dispatch(all_grads)).astype(BF16)
    )
    hidden_grad = jnp.einsum("emd,edh->emh", rows_scaled, w_dn, preferred_element_type=F32)
    share_down = reduced_product(rows_scaled, hidden)
    prob_part = jnp.sum(hidden_grad * hidden.astype(F32), axis=2).astype(BF16)
    gate_grad = (
        hidden_grad * up_pre * sigmoid_gate * (1.0 + gate_pre * (1.0 - sigmoid_gate))
    ).astype(BF16)
    up_grad = (hidden_grad * active).astype(BF16)
    both_grad = jnp.concatenate([gate_grad, up_grad], axis=2)
    share_both = reduced_product(rows_in, both_grad)

    row_grad = jnp.einsum("emh,edh->emd", both_grad, w_gu, preferred_element_type=F32).astype(BF16)
    row_grad = row_grad.reshape(local_experts, owners, capacity, model_width)

    def partial(slots):
        kept = jnp.stack([select[one] for one in slots])
        rows = jnp.stack([row_grad[:, one] for one in slots], axis=1)
        return jnp.einsum("nect,encd->ntd", kept, rows, preferred_element_type=F32)

    input_grad = scatter_blocks(partial, owners, BF16)
    slot_prob = prob_part.astype(F32).reshape(local_experts, owners, capacity)
    slot_prob = jnp.transpose(slot_prob, (1, 0, 2))
    token_prob = jnp.sum(jnp.where(chosen, slot_prob[:, :, :, None], 0.0), axis=2)
    probs = jnp.sum(jnp.where(hit, token_prob[:, :, :, None], 0.0), axis=1)
    probs = jnp.transpose(probs, (0, 2, 1))
    pair_probs = scatter_blocks(
        lambda slots: jnp.stack([probs[one] for one in slots]), owners, F32
    ).T
    router_grad = pair_probs - weights * jnp.sum(pair_probs, axis=1, keepdims=True)

    shares = jnp.stack(
        [share_both[:, :, :hidden_width], share_both[:, :, hidden_width:], share_down], axis=0
    )
    return (input_grad, router_grad, jnp.transpose(shares, (2, 0, 1, 3)))


def solution(mesh):
    rows = P(("dp", "expert"), None)
    experts = P(None, "expert", None)
    in_specs = (rows, rows, rows, rows, experts, experts, experts)
    out_specs = (rows, rows, P("dp", None, "expert", None))
    return jax.shard_map(
        per_device, mesh=mesh, in_specs=in_specs, out_specs=out_specs, check_vma=False
    )
```

```python
import jax
import jax.numpy as jnp
from jax import lax
from jax.experimental import pallas as pl
from jax.experimental.pallas import tpu as pltpu
from jax.sharding import PartitionSpec as P

BF16 = jnp.bfloat16
F32 = jnp.float32


def combine_weights(gate_logits):
    raised = jnp.exp(gate_logits)
    return raised / jnp.sum(raised, axis=1, keepdims=True)

LINE = 4


def add(*terms):
    total = terms[0].astype(F32)
    for term in terms[1:]:
        total = total + term.astype(F32)
    return total


def gather_kernel(count, *refs):
    blocks, wholes = refs[:count], refs[count : 2 * count]
    own_sem, send_sem, recv_sem = refs[2 * count :]
    me = lax.axis_index("expert")
    place, column = me // 2, me % 2
    above, below, beside = me + 2, me - 2, place * 2 + 1 - column
    has_above, has_below = place < LINE - 1, place > 0

    barrier = pltpu.get_barrier_semaphore()

    def greet(other):
        pl.semaphore_signal(
            barrier, inc=1, device_id={"expert": other}, device_id_type=pl.DeviceIdType.MESH
        )

    greet(beside)
    pl.when(has_above)(lambda: greet(above))
    pl.when(has_below)(lambda: greet(below))
    neighbours = 1 + has_above.astype(jnp.int32) + has_below.astype(jnp.int32)
    pl.semaphore_wait(barrier, neighbours)

    def copy(array, block, first, other, way):
        source = blocks[array] if first else wholes[array].at[block]
        return pltpu.make_async_remote_copy(
            src_ref=source,
            dst_ref=wholes[array].at[block],
            send_sem=send_sem.at[array, block // 2, way],
            recv_sem=recv_sem.at[array, block],
            device_id={"expert": other},
            device_id_type=pl.DeviceIdType.MESH,
        )

    def arrived(array, block):
        copy(array, block, False, beside, 2).wait_recv()

    own = [pltpu.make_async_copy(blocks[i], wholes[i].at[me], own_sem.at[i]) for i in range(count)]
    for i in range(count):
        pl.when(has_above)(lambda i=i: copy(i, me, True, above, 0).start())
        pl.when(has_below)(lambda i=i: copy(i, me, True, below, 1).start())
        copy(i, me, True, beside, 2).start()
    for one in own:
        one.start()
    for step in range(1, LINE):
        for i in range(count):

            @pl.when(place >= step)
            def _():
                block = me - 2 * step
                arrived(i, block)
                pl.when(has_above)(lambda: copy(i, block, False, above, 0).start())
                copy(i, block, False, beside, 2).start()

            @pl.when(place + step < LINE)
            def _():
                block = me + 2 * step
                arrived(i, block)
                pl.when(has_below)(lambda: copy(i, block, False, below, 1).start())
                copy(i, block, False, beside, 2).start()

    for one in own:
        one.wait()
    for i in range(count):
        for at in range(LINE):
            arrived(i, at * 2 + 1 - column)
            block = at * 2 + column
            copy(i, block, False, beside, 2).wait_send()
            pl.when(jnp.logical_and(has_above, at <= place))(
                lambda: copy(i, block, False, above, 0).wait_send()
            )
            pl.when(jnp.logical_and(has_below, at >= place))(
                lambda: copy(i, block, False, below, 1).wait_send()
            )


def gather_blocks(blocks, owners):
    if owners != 2 * LINE:
        return [lax.all_gather(block, "expert", axis=0) for block in blocks]
    count = len(blocks)
    return pl.pallas_call(
        lambda *refs: gather_kernel(count, *refs),
        out_shape=[jax.ShapeDtypeStruct((owners,) + one.shape, one.dtype) for one in blocks],
        in_specs=[pl.BlockSpec(memory_space=pl.ANY)] * count,
        out_specs=[pl.BlockSpec(memory_space=pl.ANY)] * count,
        scratch_shapes=[
            pltpu.SemaphoreType.DMA((count,)),
            pltpu.SemaphoreType.DMA((count, LINE, 3)),
            pltpu.SemaphoreType.DMA((count, owners)),
        ],
        compiler_params=pltpu.CompilerParams(collective_id=0, has_side_effects=True),
    )(*blocks)


def scatter_blocks(part_of, owners, dtype):
    if owners != 2 * LINE:
        parts = part_of(list(range(owners))).astype(dtype)
        return lax.psum_scatter(parts, "expert", scatter_dimension=0, tiled=False)
    swap = [(i, i ^ 1) for i in range(owners)]
    column = {}
    for pair in ((1, 3), (2, 0)):
        there = part_of([LINE + one for one in pair]).astype(dtype)
        back = lax.ppermute(there, "expert", swap)
        both = add(part_of(list(pair)), back)
        column[pair[0]], column[pair[1]] = both[0], both[1]
    ups, downs = None, None
    for step in range(1, LINE):
        up = [(i, i + 2) for i in range(owners - 2) if i // 2 + LINE - step <= LINE - 1]
        down = [(i, i - 2) for i in range(2, owners) if i // 2 >= LINE - step]
        send_up = column[step] if ups is None else add(column[step], ups)
        send_down = column[LINE - step] if downs is None else add(column[LINE - step], downs)
        ups = lax.ppermute(send_up.astype(dtype), "expert", up)
        downs = lax.ppermute(send_down.astype(dtype), "expert", down)
    return add(column[0], ups, downs).astype(dtype)


def over_core(part):
    return lax.ppermute(part.astype(BF16), "dp", [(0, 1), (1, 0), (2, 3), (3, 2)])


def over_chip(part):
    return lax.ppermute(part.astype(BF16), "dp", [(0, 2), (2, 0), (1, 3), (3, 1)])


def per_device(tokens_in, out_grad, gate_logits, route_ids, w_gate, w_up, w_down):
    tok_rows, model_width = tokens_in.shape
    topk_count = route_ids.shape[1]
    local_experts = w_gate.shape[1]
    hidden_width = w_gate.shape[2]
    owners = lax.axis_size("expert")
    expert_count = local_experts * owners
    capacity = 9 * tok_rows * topk_count // (8 * expert_count)
    row_count = owners * capacity
    weights = combine_weights(gate_logits)

    meta = jnp.concatenate([weights.T, route_ids.T.astype(F32)], axis=0)
    meta, all_tokens, all_grads = gather_blocks([meta, tokens_in, out_grad], owners)
    meta = jnp.transpose(meta, (0, 2, 1))

    all_weights = meta[:, :, :topk_count]
    all_ids = meta[:, :, topk_count:].astype(jnp.int32)
    mine = lax.axis_index("expert") * local_experts + jnp.arange(local_experts, dtype=jnp.int32)
    hit = all_ids[:, None, :, :] == mine[None, :, None, None]
    named = jnp.any(hit, axis=3)
    pair_weight = jnp.sum(jnp.where(hit, all_weights[:, None], 0.0), axis=3)
    earlier = (
        jnp.arange(tok_rows, dtype=jnp.int32)[:, None]
        < jnp.arange(tok_rows, dtype=jnp.int32)[None, :]
    ).astype(BF16)
    rank = jnp.einsum("nes,st->net", named.astype(BF16), earlier, preferred_element_type=F32)
    rank = jnp.where(named, rank.astype(jnp.int32), -1)
    chosen = rank[:, :, None, :] == jnp.arange(capacity, dtype=jnp.int32)[None, None, :, None]
    select = lax.optimization_barrier(chosen.astype(BF16))
    slot_weight = jnp.sum(jnp.where(chosen, pair_weight[:, :, None, :], 0.0), axis=3)

    def dispatch(blocks):
        return jnp.einsum("nect,ntd->necd", select, blocks, preferred_element_type=F32)

    def expert_major(rows):
        return jnp.transpose(rows, (1, 0, 2, 3)).reshape(local_experts, row_count, rows.shape[3])

    rows_in = expert_major(dispatch(all_tokens).astype(BF16))
    gate_pre = jnp.einsum("emd,deh->emh", rows_in, w_gate, preferred_element_type=F32)
    up_pre = jnp.einsum("emd,deh->emh", rows_in, w_up, preferred_element_type=F32)
    sigmoid_gate = jax.nn.sigmoid(gate_pre)
    active = gate_pre * sigmoid_gate
    hidden = (active * up_pre).astype(BF16)

    rows_scaled = expert_major(
        (slot_weight[:, :, :, None] * dispatch(all_grads)).astype(BF16)
    )
    hidden_grad = jnp.einsum("emd,deh->emh", rows_scaled, w_down, preferred_element_type=F32)
    prob_part = jnp.sum(hidden_grad * hidden.astype(F32), axis=2).astype(BF16)
    gate_grad = (
        hidden_grad * up_pre * sigmoid_gate * (1.0 + gate_pre * (1.0 - sigmoid_gate))
    ).astype(BF16)
    up_grad = (hidden_grad * active).astype(BF16)
    both_grad = jnp.concatenate([gate_grad, up_grad], axis=2)

    group = lax.axis_index("dp")
    chip, core = group // 2, group % 2
    width = model_width // 4

    def product(rows, grads, to_chip, to_core):
        part = lax.dynamic_slice_in_dim(rows, (to_chip * 2 + to_core) * width, width, axis=2)
        return jnp.einsum("emd,emh->edh", part, grads, preferred_element_type=F32)

    far_down = over_core(product(rows_scaled, hidden, 1 - chip, 1 - core))
    far_both = over_core(product(rows_in, both_grad, 1 - chip, 1 - core))
    far_down = add(product(rows_scaled, hidden, 1 - chip, core), far_down).astype(BF16)
    far_both = add(product(rows_in, both_grad, 1 - chip, core), far_both).astype(BF16)
    far_down, far_both, gate_grad, up_grad = lax.optimization_barrier(
        (far_down, far_both, gate_grad, up_grad)
    )
    far_down, far_both = over_chip(far_down), over_chip(far_both)
    near_down = over_core(product(rows_scaled, hidden, chip, 1 - core))
    near_both = over_core(product(rows_in, both_grad, chip, 1 - core))
    near_down = add(product(rows_scaled, hidden, chip, core), near_down).astype(BF16)
    near_both = add(product(rows_in, both_grad, chip, core), near_both).astype(BF16)
    share_down = add(near_down, far_down).astype(BF16)
    share_both = add(near_both, far_both).astype(BF16)

    row_grad = (
        jnp.einsum("emh,deh->emd", gate_grad, w_gate, preferred_element_type=F32)
        + jnp.einsum("emh,deh->emd", up_grad, w_up, preferred_element_type=F32)
    ).astype(BF16)
    row_grad = row_grad.reshape(local_experts, owners, capacity, model_width)

    me = lax.axis_index("expert")

    def block_at(slot):
        if owners != 2 * LINE:
            return slot
        place = lax.rem(me // 2 + LINE - slot % LINE, LINE)
        return place * 2 + (me + slot // LINE) % 2

    def pick(array, slots, axis):
        return jnp.concatenate(
            [lax.dynamic_slice_in_dim(array, block_at(one), 1, axis) for one in slots], axis
        )

    def partial(slots):
        return jnp.einsum(
            "nect,encd->ntd", pick(select, slots, 0), pick(row_grad, slots, 1),
            preferred_element_type=F32,
        )

    input_grad = scatter_blocks(partial, owners, BF16)
    slot_prob = prob_part.astype(F32).reshape(local_experts, owners, capacity)
    slot_prob = jnp.transpose(slot_prob, (1, 0, 2))
    token_prob = jnp.sum(jnp.where(chosen, slot_prob[:, :, :, None], 0.0), axis=2)
    probs = jnp.sum(jnp.where(hit, token_prob[:, :, :, None], 0.0), axis=1)
    probs = jnp.transpose(probs, (0, 2, 1))
    pair_probs = scatter_blocks(
        lambda slots: pick(probs, slots, 0), owners, F32
    ).T
    router_grad = pair_probs - weights * jnp.sum(pair_probs, axis=1, keepdims=True)

    shares = jnp.stack(
        [share_both[:, :, :hidden_width], share_both[:, :, hidden_width:], share_down], axis=0
    )
    return (input_grad, router_grad, jnp.transpose(shares, (2, 0, 1, 3)))


def solution(mesh):
    rows = P(("dp", "expert"), None)
    experts = P(None, "expert", None)
    in_specs = (rows, rows, rows, rows, experts, experts, experts)
    out_specs = (rows, rows, P("dp", None, "expert", None))
    return jax.shard_map(
        per_device, mesh=mesh, in_specs=in_specs, out_specs=out_specs, check_vma=False
    )
```

```python
import jax
import jax.numpy as jnp
from jax import lax
from jax.experimental import pallas as pl
from jax.experimental.pallas import tpu as pltpu
from jax.sharding import PartitionSpec as P

BF16 = jnp.bfloat16
F32 = jnp.float32


def combine_weights(gate_logits):
    raised = jnp.exp(gate_logits)
    return raised / jnp.sum(raised, axis=1, keepdims=True)

LINE = 4


def add(*terms):
    total = terms[0].astype(F32)
    for term in terms[1:]:
        total = total + term.astype(F32)
    return total


def gather_kernel(count, *refs):
    blocks, wholes = refs[:count], refs[count : 2 * count]
    own_sem, send_sem, recv_sem = refs[2 * count :]
    me = lax.axis_index("expert")
    place, column = me // 2, me % 2
    above, below, beside = me + 2, me - 2, place * 2 + 1 - column
    has_above, has_below = place < LINE - 1, place > 0

    barrier = pltpu.get_barrier_semaphore()

    def greet(other):
        pl.semaphore_signal(
            barrier, inc=1, device_id={"expert": other}, device_id_type=pl.DeviceIdType.MESH
        )

    greet(beside)
    pl.when(has_above)(lambda: greet(above))
    pl.when(has_below)(lambda: greet(below))
    neighbours = 1 + has_above.astype(jnp.int32) + has_below.astype(jnp.int32)
    pl.semaphore_wait(barrier, neighbours)

    def copy(array, block, first, other, way):
        source = blocks[array] if first else wholes[array].at[block]
        return pltpu.make_async_remote_copy(
            src_ref=source,
            dst_ref=wholes[array].at[block],
            send_sem=send_sem.at[array, block // 2, way],
            recv_sem=recv_sem.at[array, block],
            device_id={"expert": other},
            device_id_type=pl.DeviceIdType.MESH,
        )

    def arrived(array, block):
        copy(array, block, False, beside, 2).wait_recv()

    own = [pltpu.make_async_copy(blocks[i], wholes[i].at[me], own_sem.at[i]) for i in range(count)]
    for i in range(count):
        pl.when(has_above)(lambda i=i: copy(i, me, True, above, 0).start())
        pl.when(has_below)(lambda i=i: copy(i, me, True, below, 1).start())
        copy(i, me, True, beside, 2).start()
    for one in own:
        one.start()
    for step in range(1, LINE):
        for i in range(count):

            @pl.when(place >= step)
            def _():
                block = me - 2 * step
                arrived(i, block)
                pl.when(has_above)(lambda: copy(i, block, False, above, 0).start())
                copy(i, block, False, beside, 2).start()

            @pl.when(place + step < LINE)
            def _():
                block = me + 2 * step
                arrived(i, block)
                pl.when(has_below)(lambda: copy(i, block, False, below, 1).start())
                copy(i, block, False, beside, 2).start()

    for one in own:
        one.wait()
    for i in range(count):
        for at in range(LINE):
            arrived(i, at * 2 + 1 - column)
            block = at * 2 + column
            copy(i, block, False, beside, 2).wait_send()
            pl.when(jnp.logical_and(has_above, at <= place))(
                lambda: copy(i, block, False, above, 0).wait_send()
            )
            pl.when(jnp.logical_and(has_below, at >= place))(
                lambda: copy(i, block, False, below, 1).wait_send()
            )


def gather_blocks(blocks, owners):
    if owners != 2 * LINE:
        return [lax.all_gather(block, "expert", axis=0) for block in blocks]
    count = len(blocks)
    return pl.pallas_call(
        lambda *refs: gather_kernel(count, *refs),
        out_shape=[jax.ShapeDtypeStruct((owners,) + one.shape, one.dtype) for one in blocks],
        in_specs=[pl.BlockSpec(memory_space=pl.ANY)] * count,
        out_specs=[pl.BlockSpec(memory_space=pl.ANY)] * count,
        scratch_shapes=[
            pltpu.SemaphoreType.DMA((count,)),
            pltpu.SemaphoreType.DMA((count, LINE, 3)),
            pltpu.SemaphoreType.DMA((count, owners)),
        ],
        compiler_params=pltpu.CompilerParams(collective_id=0, has_side_effects=True),
    )(*blocks)


def scatter_blocks(part_of, owners, dtype):
    if owners != 2 * LINE:
        parts = part_of(list(range(owners))).astype(dtype)
        return lax.psum_scatter(parts, "expert", scatter_dimension=0, tiled=False)
    swap = [(i, i ^ 1) for i in range(owners)]
    column = {}
    for pair in ((1, 3), (2, 0)):
        there = part_of([LINE + one for one in pair]).astype(dtype)
        back = lax.ppermute(there, "expert", swap)
        both = add(part_of(list(pair)), back)
        column[pair[0]], column[pair[1]] = both[0], both[1]
    ups, downs = None, None
    for step in range(1, LINE):
        up = [(i, i + 2) for i in range(owners - 2) if i // 2 + LINE - step <= LINE - 1]
        down = [(i, i - 2) for i in range(2, owners) if i // 2 >= LINE - step]
        send_up = column[step] if ups is None else add(column[step], ups)
        send_down = column[LINE - step] if downs is None else add(column[LINE - step], downs)
        ups = lax.ppermute(send_up.astype(dtype), "expert", up)
        downs = lax.ppermute(send_down.astype(dtype), "expert", down)
    return add(column[0], ups, downs).astype(dtype)


def over_core(part):
    return lax.ppermute(part.astype(BF16), "dp", [(0, 1), (1, 0), (2, 3), (3, 2)])


def over_chip(part):
    return lax.ppermute(part.astype(BF16), "dp", [(0, 2), (2, 0), (1, 3), (3, 1)])


def per_device(tokens_in, out_grad, gate_logits, route_ids, w_gate, w_up, w_down):
    tok_rows, model_width = tokens_in.shape
    topk_count = route_ids.shape[1]
    local_experts = w_gate.shape[1]
    hidden_width = w_gate.shape[2]
    owners = lax.axis_size("expert")
    expert_count = local_experts * owners
    capacity = 9 * tok_rows * topk_count // (8 * expert_count)
    row_count = owners * capacity
    weights = combine_weights(gate_logits)

    meta = jnp.concatenate([weights.T, route_ids.T.astype(F32)], axis=0)
    meta, all_tokens, all_grads = gather_blocks([meta, tokens_in, out_grad], owners)
    meta = jnp.transpose(meta, (0, 2, 1))

    all_weights = meta[:, :, :topk_count]
    all_ids = meta[:, :, topk_count:].astype(jnp.int32)
    mine = lax.axis_index("expert") * local_experts + jnp.arange(local_experts, dtype=jnp.int32)
    hit = all_ids[:, None, :, :] == mine[None, :, None, None]
    named = jnp.any(hit, axis=3)
    pair_weight = jnp.sum(jnp.where(hit, all_weights[:, None], 0.0), axis=3)
    earlier = (
        jnp.arange(tok_rows, dtype=jnp.int32)[:, None]
        < jnp.arange(tok_rows, dtype=jnp.int32)[None, :]
    ).astype(BF16)
    rank = jnp.einsum("nes,st->net", named.astype(BF16), earlier, preferred_element_type=F32)
    rank = jnp.where(named, rank.astype(jnp.int32), -1)
    chosen = rank[:, :, None, :] == jnp.arange(capacity, dtype=jnp.int32)[None, None, :, None]
    select = lax.optimization_barrier(chosen.astype(BF16))
    slot_weight = jnp.sum(jnp.where(chosen, pair_weight[:, :, None, :], 0.0), axis=3)

    def dispatch(blocks):
        return jnp.einsum("nect,ntd->necd", select, blocks, preferred_element_type=F32)

    def expert_major(rows):
        return jnp.transpose(rows, (1, 0, 2, 3)).reshape(local_experts, row_count, rows.shape[3])

    rows_in = expert_major(dispatch(all_tokens).astype(BF16))
    gate_pre = jnp.einsum("emd,deh->emh", rows_in, w_gate, preferred_element_type=F32)
    up_pre = jnp.einsum("emd,deh->emh", rows_in, w_up, preferred_element_type=F32)
    sigmoid_gate = jax.nn.sigmoid(gate_pre)
    active = gate_pre * sigmoid_gate
    hidden = (active * up_pre).astype(BF16)

    rows_scaled = expert_major(
        (slot_weight[:, :, :, None] * dispatch(all_grads)).astype(BF16)
    )
    hidden_grad = jnp.einsum("emd,deh->emh", rows_scaled, w_down, preferred_element_type=F32)
    prob_part = jnp.sum(hidden_grad * hidden.astype(F32), axis=2).astype(BF16)
    gate_grad = (
        hidden_grad * up_pre * sigmoid_gate * (1.0 + gate_pre * (1.0 - sigmoid_gate))
    ).astype(BF16)
    up_grad = (hidden_grad * active).astype(BF16)
    both_grad = jnp.concatenate([gate_grad, up_grad], axis=2)

    group = lax.axis_index("dp")
    chip, core = group // 2, group % 2
    width = model_width // 4

    def product(rows, grads, to_chip, to_core):
        part = lax.dynamic_slice_in_dim(rows, (to_chip * 2 + to_core) * width, width, axis=2)
        return jnp.einsum("emd,emh->edh", part, grads, preferred_element_type=F32)

    far_down = over_core(product(rows_scaled, hidden, 1 - chip, 1 - core))
    far_both = over_core(product(rows_in, both_grad, 1 - chip, 1 - core))
    far_down = add(product(rows_scaled, hidden, 1 - chip, core), far_down).astype(BF16)
    far_both = add(product(rows_in, both_grad, 1 - chip, core), far_both).astype(BF16)
    far_down, far_both, gate_grad, up_grad = lax.optimization_barrier(
        (far_down, far_both, gate_grad, up_grad)
    )
    far_down, far_both = over_chip(far_down), over_chip(far_both)
    near_down = over_core(product(rows_scaled, hidden, chip, 1 - core))
    near_both = over_core(product(rows_in, both_grad, chip, 1 - core))
    near_down = add(product(rows_scaled, hidden, chip, core), near_down).astype(BF16)
    near_both = add(product(rows_in, both_grad, chip, core), near_both).astype(BF16)

    row_grad = (
        jnp.einsum("emh,deh->emd", gate_grad, w_gate, preferred_element_type=F32)
        + jnp.einsum("emh,deh->emd", up_grad, w_up, preferred_element_type=F32)
    ).astype(BF16)
    far_down, row_grad = lax.optimization_barrier((far_down, row_grad))
    share_down = add(near_down, far_down).astype(BF16)
    share_both = add(near_both, far_both).astype(BF16)
    row_grad = row_grad.reshape(local_experts, owners, capacity, model_width)

    me = lax.axis_index("expert")

    def block_at(slot):
        if owners != 2 * LINE:
            return slot
        place = lax.rem(me // 2 + LINE - slot % LINE, LINE)
        return place * 2 + (me + slot // LINE) % 2

    def pick(array, slots, axis):
        return jnp.concatenate(
            [lax.dynamic_slice_in_dim(array, block_at(one), 1, axis) for one in slots], axis
        )

    def partial(slots):
        return jnp.einsum(
            "nect,encd->ntd", pick(select, slots, 0), pick(row_grad, slots, 1),
            preferred_element_type=F32,
        )

    input_grad = scatter_blocks(partial, owners, BF16)
    slot_prob = prob_part.astype(F32).reshape(local_experts, owners, capacity)
    slot_prob = jnp.transpose(slot_prob, (1, 0, 2))
    token_prob = jnp.sum(jnp.where(chosen, slot_prob[:, :, :, None], 0.0), axis=2)
    probs = jnp.sum(jnp.where(hit, token_prob[:, :, :, None], 0.0), axis=1)
    probs = jnp.transpose(probs, (0, 2, 1))
    pair_probs = scatter_blocks(
        lambda slots: pick(probs, slots, 0), owners, F32
    ).T
    router_grad = pair_probs - weights * jnp.sum(pair_probs, axis=1, keepdims=True)

    shares = jnp.stack(
        [share_both[:, :, :hidden_width], share_both[:, :, hidden_width:], share_down], axis=0
    )
    return (input_grad, router_grad, jnp.transpose(shares, (2, 0, 1, 3)))


def solution(mesh):
    rows = P(("dp", "expert"), None)
    experts = P(None, "expert", None)
    in_specs = (rows, rows, rows, rows, experts, experts, experts)
    out_specs = (rows, rows, P("dp", None, "expert", None))
    return jax.shard_map(
        per_device, mesh=mesh, in_specs=in_specs, out_specs=out_specs, check_vma=False
    )
```
